256 devices in a mesh: ctx: 128 (over z, x, y), head: 2 (over core).
Axes of the slice: x: 4, y: 4, z: 8, core: 2. Of those that a mesh axis runs over, the one named last changes fastest.
Arguments:
- queries: bfloat16 [65536, 512], P('ctx', 'head'), may hold values from -48 to 48
- keys: bfloat16 [65536, 128], P('ctx'), may hold values from -6 to 6
- values: bfloat16 [65536, 128], P('ctx'), may hold values from -6 to 6
- out_grad: bfloat16 [65536, 512], P('ctx', 'head'), may hold values from -6 to 6
- lengths: int32 [64], replicated, may hold values from 1 to 3584, 65536 in all
Outputs:
- attended: bfloat16 [65536, 512], P('ctx', 'head')
- query_grad: bfloat16 [65536, 512], P('ctx', 'head')
- key_grad: bfloat16 [65536, 128], P(('ctx', 'head'))
- value_grad: bfloat16 [65536, 128], P(('ctx', 'head'))
The draws below stay inside these ranges and needn't reach their ends.
Inputs may be any that keep to these rules, and one draw needn't show every extreme that they name: The lengths sum to 65536, and the largest is exactly 3584.
All inputs are finite; a program needn't handle non-finite values.
Results may differ from the reference program's by a relative error of at most 0.038.
Values may be sent and summed in bfloat16 or wider, within the bound.
A program may use at most 128 MiB of HBM per device.

```python
import math
import jax
import jax.numpy as jnp
import numpy as np
from jax import lax

TOK_DEV = 512
HD = 128
HEADS = 4
WIN = 8
MOST = 3584
TOKENS = 65536
DOCS = 64


def shared_fields(key):
    normal_part = jax.random.normal(key, (TOKENS, HD), jnp.float32)
    even_part = jax.random.uniform(jax.random.fold_in(key, 11), (TOKENS, HD), jnp.float32, -2.0, 2.0)
    noise_part = jax.random.normal(jax.random.fold_in(key, 12), (TOKENS, HD), jnp.float32)
    return (normal_part, even_part, noise_part)


def key_rows(fields):
    normal_part, even_part, noise_part = fields
    base_rows = jnp.clip(normal_part, -6.0, 6.0)
    paired = (jnp.arange(TOKENS) % 32 == 1)[:, None]
    tied = base_rows
    return jnp.where(paired, tied, base_rows)


def draw_keys(key, part):
    fields = shared_fields(key)
    rows_out = key_rows(fields)
    return rows_out.astype(jnp.bfloat16)


def draw_queries(key, part):
    key = jax.random.fold_in(key, 5)
    rows_out = 2.0 * jnp.clip(jax.random.normal(key, (TOKENS, HEADS * HD), jnp.float32), -6.0, 6.0)
    return rows_out.astype(jnp.bfloat16)


def level_of(stream_key, dims, pieces, low, high):
    def one(dim, parts):
        draws = jax.random.uniform(jax.random.fold_in(jax.random.fold_in(stream_key, 6), dim), (parts,), jnp.float32, low / len(pieces), high / len(pieces))
        return jnp.repeat(jnp.exp(draws), dims[dim] // parts).reshape((-1,) + (1,) * (len(dims) - dim - 1))

    factor_of = one(*pieces[0])
    for cut in pieces[1:]:
        factor_of = factor_of * one(*cut)
    return factor_of


def split_up(number_of, total, limit, lean):
    loads = [(1 << 20) // math.isqrt(standing ** lean) + 1 for standing in range(2, number_of + 1)]
    spare, holding = total - limit - (number_of - 1), [1] * (number_of - 1)
    while spare > 0:
        free = [i for i in range(number_of - 1) if holding[i] < limit]
        whole, remaining = sum([loads[i] for i in free]), spare
        for i in free:
            more = min(limit - holding[i], max(1, remaining * loads[i] // whole), spare)
            holding[i] = holding[i] + more
            spare = spare - more
    return np.array([limit] + holding)


def ragged(key, number_of, total, most, slope):
    if number_of == 2:
        one = jax.random.randint(key, (), max(1, total - most), min(most, total - 1) + 1)
        return jnp.stack([one, total - one])
    tallies = jnp.asarray(split_up(number_of, total, most, slope), jnp.int32)
    couples = (number_of - 1) // 2
    giver, receiver = tallies[1:1 + 2 * couples:2], tallies[2:2 + 2 * couples:2]
    margin = jnp.minimum(giver - 1, most - receiver)
    shifted = jax.random.randint(jax.random.fold_in(key, 1), (couples,), 0, 1 << 20) % (margin + 1)
    tallies = tallies.at[1:1 + 2 * couples:2].set(giver - shifted).at[2:2 + 2 * couples:2].set(receiver + shifted)
    return tallies[jax.random.permutation(jax.random.fold_in(key, 2), number_of)]


def gaussian(rng, shape, scale, most, cuts=(), kind=jnp.bfloat16):
    loudness = level_of(rng, shape, cuts, -0.22, 0.18) if cuts else 1.0
    values = jax.random.normal(rng, shape, jnp.float32) * scale * loudness
    return jnp.minimum(jnp.maximum(values, -most), most).astype(kind)


def setup_inputs(seed: int = 0) -> dict:
    splits = jax.random.split(jax.random.key(seed), 6)
    return {
        "queries": draw_queries(jax.random.fold_in(splits[5], 71), 0),
        "keys": draw_keys(jax.random.fold_in(splits[5], 71), 0),
        "values": gaussian(splits[2], (TOKENS, HD), 1.0, 6.0, ((0, 128),)),
        "out_grad": gaussian(splits[3], (TOKENS, HEADS * HD), 1.0, 6.0, ((0, 128), (1, 2))),
        "lengths": ragged(splits[4], DOCS, TOKENS, MOST, 2).astype(jnp.int32),
    }


neg_big = -1e+30

def doc_begin(lengths, positions):
    ends = jnp.cumsum(lengths).astype(jnp.int32)
    begins = ends - lengths.astype(jnp.int32)
    inside = begins[None, :] <= positions[:, None]
    return lax.optimization_barrier(jnp.max(jnp.where(inside, begins[None, :], 0), axis=1)).astype(jnp.int32)

def reference(queries, keys, values, out_grad, lengths):
    head_width = keys.shape[1]
    head_count = queries.shape[1] // head_width
    tok_rows = TOK_DEV
    reach = (WIN - 1) * tok_rows
    span_rows = WIN * tok_rows
    block_count = keys.shape[0] // tok_rows
    score_scale = 1.0 / math.sqrt(head_width)
    zero_rows = jnp.zeros((reach, head_width), keys.dtype)
    padded_keys = jnp.concatenate([zero_rows, keys], axis=0)
    padded_values = jnp.concatenate([zero_rows, values], axis=0)
    grad_init = jnp.zeros((keys.shape[0] + reach, head_width), jnp.float32)
    highest = lax.Precision.HIGHEST

    def one_block(state_in, block_index):
        key_total, value_total = state_in
        first_row = (block_index * tok_rows).astype(jnp.int32)
        query_heads = lax.dynamic_slice_in_dim(queries, first_row, tok_rows, 0).reshape(tok_rows, head_count, head_width).astype(jnp.float32)
        grad_heads = lax.dynamic_slice_in_dim(out_grad, first_row, tok_rows, 0).reshape(tok_rows, head_count, head_width).astype(jnp.float32)
        key_window = lax.dynamic_slice_in_dim(padded_keys, first_row, span_rows, 0).astype(jnp.float32)
        value_window = lax.dynamic_slice_in_dim(padded_values, first_row, span_rows, 0).astype(jnp.float32)
        query_pos = first_row + jnp.arange(tok_rows, dtype=jnp.int32)
        query_begin = doc_begin(lengths, query_pos)
        key_pos = first_row - reach + jnp.arange(span_rows, dtype=jnp.int32)
        allowed = (key_pos[None, :] >= query_begin[:, None]) & (key_pos[None, :] <= query_pos[:, None])
        scores = jnp.einsum('rhd,cd->hrc', query_heads, key_window, precision=highest) * score_scale
        scores = jnp.where(allowed[None], scores, neg_big)
        row_max = lax.optimization_barrier(jnp.max(scores, axis=-1, keepdims=True))
        log_total = row_max + jnp.log(lax.optimization_barrier(jnp.sum(jnp.exp(scores - row_max), axis=-1, keepdims=True)))
        weights = jnp.exp(scores - log_total)
        weights_low = lax.optimization_barrier(weights.astype(jnp.bfloat16)).astype(jnp.float32)
        attended = jnp.einsum('hrc,cd->rhd', weights_low, value_window, precision=highest).astype(jnp.bfloat16)
        attended_wide = lax.optimization_barrier(attended).astype(jnp.float32)
        row_delta = lax.optimization_barrier(jnp.sum(grad_heads * attended_wide, axis=-1)).T
        prob_grad = jnp.einsum('rhd,cd->hrc', grad_heads, value_window, precision=highest)
        score_grad = (weights * (prob_grad - row_delta[:, :, None])).astype(jnp.bfloat16)
        score_low = lax.optimization_barrier(score_grad).astype(jnp.float32)
        query_grad = jnp.einsum('hrc,cd->rhd', score_low, key_window, precision=highest) * score_scale
        key_part = jnp.einsum('hrc,rhd->cd', score_low, query_heads, precision=highest) * score_scale
        value_part = jnp.einsum('hrc,rhd->cd', weights_low, grad_heads, precision=highest)
        key_total = lax.dynamic_update_slice_in_dim(key_total, lax.dynamic_slice_in_dim(key_total, first_row, span_rows, 0) + key_part, first_row, 0)
        value_total = lax.dynamic_update_slice_in_dim(value_total, lax.dynamic_slice_in_dim(value_total, first_row, span_rows, 0) + value_part, first_row, 0)
        outputs = (attended.reshape(tok_rows, head_count * head_width), query_grad.astype(jnp.bfloat16).reshape(tok_rows, head_count * head_width))
        return ((key_total, value_total), outputs)
    totals, outputs = lax.scan(one_block, (grad_init, grad_init), jnp.arange(block_count, dtype=jnp.int32))
    attended_all = outputs[0].reshape(keys.shape[0], head_count * head_width)
    query_all = outputs[1].reshape(keys.shape[0], head_count * head_width)
    key_grad = totals[0][reach:].astype(jnp.bfloat16)
    value_grad = totals[1][reach:].astype(jnp.bfloat16)
    return (attended_all, query_all, key_grad, value_grad)
```

```python
import functools
import math

import jax
import jax.numpy as jnp
from jax import lax
from jax.experimental import pallas as pl
from jax.experimental.pallas import tpu as pltpu
from jax.sharding import PartitionSpec as P

MESH = pl.DeviceIdType.MESH
WIN = 8
LINE = 4
NEG = -1e30


def dot_nn(a, b):
    return lax.dot_general(a, b, (((1,), (0,)), ((), ())), preferred_element_type=jnp.float32)


def dot_nt(a, b):
    return lax.dot_general(a, b, (((1,), (1,)), ((), ())), preferred_element_type=jnp.float32)


def kernel(
    shards, docs, len_ref, q_ref, k_ref, v_ref, g_ref,
    att_ref, dq_ref, dk_ref, dv_ref,
    win, p_buf, ds_buf, m_buf, m_now, l_now, acc, delta, begin_buf, qt, gt,
    mine, sib_out, sib_in, out_buf, relay_in, back_in,
    a_send, a_recv, relay_send, fwd_send, fwd_recv, sum_send, sum_recv,
    back_send, back_recv, col_send, col_recv, line_send, line_recv,
):
    me = lax.axis_index("ctx")
    core = lax.axis_index("head")
    tok, width = k_ref.shape
    heads = q_ref.shape[1] // width
    half = tok // 2
    tile = min(256, tok)
    scale = 1.0 / math.sqrt(width)
    scale2 = scale * math.log2(math.e)
    line = me // LINE
    place = me % LINE
    my_rows = pl.ds(pl.multiple_of(core * half, half), half)
    sib_rows = pl.ds(pl.multiple_of((1 - core) * half, half), half)
    sibling = (me, 1 - core)

    def remote(src, dst, send, recv, device):
        return pltpu.make_async_remote_copy(
            src_ref=src, dst_ref=dst, send_sem=send, recv_sem=recv, device_id=device, device_id_type=MESH
        )

    def ahead(step):
        return me + step + LINE * ((place + step) // LINE)

    def behind(step):
        return me - step - LINE * ((LINE - 1 - place + step) // LINE)

    def on_line(step):
        return line * LINE + (place + step + LINE) % LINE

    def distance(slot):
        step = slot % LINE
        wrap = (LINE - 1 - place + step) // LINE
        late = slot // LINE
        return step + LINE * (wrap + late - 2 * wrap * late)

    def exists(slot):
        return me - distance(slot) >= 0

    has_next = me + LINE < shards
    has_prev = line >= 1

    win[0, :, 0:width] = k_ref[...]
    win[0, :, width:] = v_ref[...]

    @pl.when(line < 2)
    def _():
        for slot in range(1, WIN):
            win[slot] = jnp.zeros(win.shape[1:], win.dtype)

    barrier = pltpu.get_barrier_semaphore()

    def greet(device):
        pl.semaphore_signal(barrier, inc=1, device_id=device, device_id_type=MESH)

    greet(sibling)
    for step in range(1, LINE):
        greet((on_line(step), core))
    for step in range(1, LINE):
        up, down = ahead(step), behind(step)
        far_up = jnp.logical_and(place + step >= LINE, up < shards)
        far_down = jnp.logical_and(place < step, down >= 0)

        @pl.when(far_up)
        def _():
            greet((up, core))

        @pl.when(far_down)
        def _():
            greet((down, core))


    @pl.when(has_next)
    def _():
        greet((me + LINE, core))

    @pl.when(has_prev)
    def _():
        greet((me - LINE, core))

    lines = shards // LINE
    near = (line + lines - 1) // lines + 1 - (line + 1) // lines
    far = place * (1 - (line + 2) // lines) + (LINE - 1 - place) * ((line + lines - 2) // lines)
    pl.semaphore_wait(barrier, LINE + near + far)

    def block_send(slot, device):
        return remote(win.at[0, my_rows], win.at[slot, my_rows], a_send.at[slot], a_recv.at[slot], (device, core))

    def relay_copy(step):
        return remote(
            win.at[LINE, my_rows], win.at[LINE + step, my_rows],
            relay_send.at[step], a_recv.at[LINE + step], (on_line(step), core),
        )

    @pl.when(has_next)
    def _():
        block_send(LINE, me + LINE).start()

    for step in range(1, LINE):

        @pl.when(ahead(step) < shards)
        def _():
            block_send(step, ahead(step)).start()

    for h in range(heads):
        qt[:, h * tok : (h + 1) * tok] = q_ref[:, h * width : (h + 1) * width].T
        gt[:, h * tok : (h + 1) * tok] = g_ref[:, h * width : (h + 1) * width].T

    row_pos = me * tok + lax.broadcasted_iota(jnp.int32, (tok, width), 0)
    begin_buf[...] = jnp.zeros((tok, width), jnp.int32)

    def one_doc(doc, first):
        begin_buf[...] = jnp.where(first <= row_pos, first, begin_buf[...])
        return first + len_ref[doc]

    lax.fori_loop(0, docs, one_doc, jnp.int32(0))

    m_now[...] = jnp.full(m_now.shape, NEG, jnp.float32)
    l_now[...] = jnp.zeros(l_now.shape, jnp.float32)
    acc[...] = jnp.zeros(acc.shape, jnp.float32)
    tiles = tok // tile

    def rows_of(index):
        return pl.ds(pl.multiple_of(index * tile, tile), tile)

    def score_pass(slot, own):
        keys = win[slot, :, 0:width]
        vals = win[slot, :, width:]
        key_first = (me - distance(slot)) * tok

        for h in range(heads):

            def body(t, _):
                rows = rows_of(t)
                state = rows_of(t + h * tiles)
                scores = dot_nt(q_ref[rows, h * width : (h + 1) * width], keys) * scale2
                first = begin_buf[rows, 0:1] - key_first
                key_pos = lax.broadcasted_iota(jnp.int32, scores.shape, 1)
                allowed = key_pos >= first
                if own:
                    row = t * tile + lax.broadcasted_iota(jnp.int32, scores.shape, 0)
                    allowed = jnp.logical_and(allowed, key_pos <= row)
                scores = jnp.where(allowed, scores, NEG)
                old = m_now[state, :]
                new = jnp.maximum(old, jnp.max(scores, axis=1, keepdims=True))
                shrink = jnp.exp2(old - new)
                probs = jnp.exp2(scores - new[:, 0:1])
                l_now[state, :] = l_now[state, :] * shrink + jnp.sum(probs, axis=1, keepdims=True)
                m_now[state, :] = new
                m_buf[slot, state, :] = new
                low = probs.astype(jnp.bfloat16)
                p_buf[slot, state, :] = low
                acc[state, :] = acc[state, :] * shrink + dot_nn(low, vals)
                return 0

            lax.fori_loop(0, tiles, body, 0)

    score_pass(0, True)

    def arrival(slot):
        @pl.when(exists(slot))
        def _():
            piece = win.at[slot, my_rows]
            remote(piece, piece, fwd_send.at[slot], a_recv.at[slot], sibling).wait_recv()
            remote(piece, piece, fwd_send.at[slot], fwd_recv.at[slot], sibling).start()

    def arrival_end(slot):
        @pl.when(exists(slot))
        def _():
            piece = win.at[slot, sib_rows]
            remote(piece, piece, fwd_send.at[slot], fwd_recv.at[slot], sibling).wait_recv()

    @pl.when(has_prev)
    def _():
        piece = win.at[LINE, my_rows]
        remote(piece, piece, fwd_send.at[LINE], a_recv.at[LINE], sibling).wait_recv()
        for step in range(1, LINE):
            relay_copy(step).start()
        remote(piece, piece, fwd_send.at[LINE], fwd_recv.at[LINE], sibling).start()

    order = (4, 1, 2, 3, 5, 6, 7)
    for index, slot in enumerate(order):
        if index + 1 < len(order):
            arrival(order[index + 1])
        arrival_end(slot)
        score_pass(slot, False)

    for h in range(heads):

        def finish(t, _):
            rows = rows_of(t)
            state = rows_of(t + h * tiles)
            inverse = 1.0 / l_now[state, :]
            out = (acc[state, :] * inverse).astype(jnp.bfloat16)
            att_ref[rows, h * width : (h + 1) * width] = out
            grads = g_ref[rows, h * width : (h + 1) * width].astype(jnp.float32)
            total = jnp.sum(grads * out.astype(jnp.float32), axis=1, keepdims=True)
            delta[state, :] = jnp.broadcast_to(total, (tile, width))
            l_now[state, :] = inverse
            return 0

        lax.fori_loop(0, tiles, finish, 0)

    def grad_pass(slot):
        vals = win[slot, :, width:]

        for h in range(heads):

            def body(t, _):
                rows = rows_of(t)
                state = rows_of(t + h * tiles)
                factor = jnp.exp2(m_buf[slot, state, :] - m_now[state, :]) * l_now[state, :]
                probs = p_buf[slot, state, :].astype(jnp.float32) * factor[:, 0:1]
                p_buf[slot, state, :] = probs.astype(jnp.bfloat16)
                prob_grad = dot_nt(g_ref[rows, h * width : (h + 1) * width], vals)
                ds_buf[slot, state, :] = (probs * (prob_grad - delta[state, 0:1])).astype(jnp.bfloat16)
                return 0

            lax.fori_loop(0, tiles, body, 0)
        for top, left, right in ((0, qt, ds_buf), (width, gt, p_buf)):
            part = dot_nn(left[...], right[slot])
            bottom = top + width

            @pl.when(core == 0)
            def _():
                mine[slot, top:bottom, :] = part[:, 0:half]
                sib_out[slot, top:bottom, :] = part[:, half:].astype(jnp.bfloat16)

            @pl.when(core == 1)
            def _():
                mine[slot, top:bottom, :] = part[:, half:]
                sib_out[slot, top:bottom, :] = part[:, 0:half].astype(jnp.bfloat16)

    def sum_copy(slot):
        return remote(sib_out.at[slot], sib_in.at[slot], sum_send.at[slot], sum_recv.at[slot], sibling)

    def back_copy(step):
        return remote(
            out_buf.at[step], back_in.at[step], back_send.at[step], back_recv.at[step], (behind(step), core)
        )

    def line_copy(step):
        return remote(
            out_buf.at[LINE + step], relay_in.at[step], line_send.at[step], line_recv.at[step], (on_line(-step), core)
        )

    def col_copy():
        return remote(out_buf.at[LINE], back_in.at[0], col_send.at[0], col_recv.at[0], (me - LINE, core))

    def return_part(slot):
        sum_copy(slot).wait_recv()
        total = mine[slot] + sib_in[slot].astype(jnp.float32)
        mine[slot] = total
        out_buf[slot] = total.astype(jnp.bfloat16)

        if slot > LINE:

            @pl.when(has_prev)
            def _():
                line_copy(slot - LINE).start()

        if 0 < slot < LINE:

            @pl.when(exists(slot))
            def _():
                back_copy(slot).start()

    back_order = (5, 6, 7, 4, 1, 2, 3, 0)
    for index, slot in enumerate(back_order):
        grad_pass(slot)
        sum_copy(slot).start()
        if index > 0:
            return_part(back_order[index - 1])
    return_part(back_order[-1])

    @pl.when(has_prev)
    def _():
        for step in range(1, LINE):
            line_copy(step).wait_recv()
        total = mine[LINE]
        for step in range(1, LINE):
            total = total + relay_in[step].astype(jnp.float32)
        out_buf[LINE] = total.astype(jnp.bfloat16)
        col_copy().start()

    for h in range(heads):

        def query_tile(t, _):
            rows = rows_of(t)
            state = rows_of(t + h * tiles)
            total = jnp.zeros((tile, width), jnp.float32)
            for slot in range(WIN):
                total = total + dot_nn(ds_buf[slot, state, :], win[slot, :, 0:width])
            dq_ref[rows, h * width : (h + 1) * width] = (total * scale).astype(jnp.bfloat16)
            return 0

        lax.fori_loop(0, tiles, query_tile, 0)

    for step in range(1, LINE):

        @pl.when(ahead(step) < shards)
        def _():
            back_copy(step).wait_recv()
            mine[0] = mine[0] + back_in[step].astype(jnp.float32)

    @pl.when(has_next)
    def _():
        col_copy().wait_recv()
        mine[0] = mine[0] + back_in[0].astype(jnp.float32)

    dk_ref[...] = (mine[0, 0:width, :] * scale).T.astype(jnp.bfloat16)
    dv_ref[...] = mine[0, width:, :].T.astype(jnp.bfloat16)

    @pl.when(has_next)
    def _():
        block_send(LINE, me + LINE).wait_send()

    for step in range(1, LINE):

        @pl.when(ahead(step) < shards)
        def _():
            block_send(step, ahead(step)).wait_send()

    @pl.when(has_prev)
    def _():
        for step in range(1, LINE):
            relay_copy(step).wait_send()
            line_copy(step).wait_send()
        col_copy().wait_send()

    for slot in range(1, WIN):

        @pl.when(exists(slot))
        def _():
            piece = win.at[slot, my_rows]
            remote(piece, piece, fwd_send.at[slot], fwd_recv.at[slot], sibling).wait_send()

    for slot in range(WIN):
        sum_copy(slot).wait_send()

    for step in range(1, LINE):

        @pl.when(behind(step) >= 0)
        def _():
            back_copy(step).wait_send()


def solution(mesh):
    shards = mesh.shape["ctx"]

    def on_device(queries, keys, values, out_grad, lengths):
        tok, width = keys.shape
        heads = queries.shape[1] // width
        rows = heads * tok
        half = tok // 2
        bf16, f32 = jnp.bfloat16, jnp.float32
        vmem = pl.BlockSpec(memory_space=pltpu.VMEM)
        dma = pltpu.SemaphoreType.DMA
        flops = 6 * 2 * rows * WIN * tok * width
        return pl.pallas_call(
            functools.partial(kernel, shards, lengths.shape[0]),
            out_shape=(
                jax.ShapeDtypeStruct(queries.shape, bf16),
                jax.ShapeDtypeStruct(queries.shape, bf16),
                jax.ShapeDtypeStruct((half, width), bf16),
                jax.ShapeDtypeStruct((half, width), bf16),
            ),
            in_specs=[pl.BlockSpec(memory_space=pltpu.SMEM)] + [vmem] * 4,
            out_specs=(vmem,) * 4,
            scratch_shapes=[
                pltpu.VMEM((WIN, tok, 2 * width), bf16),
                pltpu.VMEM((WIN, rows, tok), bf16),
                pltpu.VMEM((WIN, rows, tok), bf16),
                pltpu.VMEM((WIN, rows, width), f32),
                pltpu.VMEM((rows, width), f32),
                pltpu.VMEM((rows, width), f32),
                pltpu.VMEM((rows, width), f32),
                pltpu.VMEM((rows, width), f32),
                pltpu.VMEM((tok, width), jnp.int32),
                pltpu.VMEM((width, rows), bf16),
                pltpu.VMEM((width, rows), bf16),
                pltpu.VMEM((WIN, 2 * width, half), f32),
                pltpu.VMEM((WIN, 2 * width, half), bf16),
                pltpu.VMEM((WIN, 2 * width, half), bf16),
                pltpu.VMEM((WIN, 2 * width, half), bf16),
                pltpu.VMEM((LINE, 2 * width, half), bf16),
                pltpu.VMEM((LINE, 2 * width, half), bf16),
                dma((WIN,)), dma((WIN,)), dma((LINE,)), dma((WIN,)), dma((WIN,)), dma((WIN,)), dma((WIN,)),
                dma((LINE,)), dma((LINE,)), dma((1,)), dma((1,)), dma((LINE,)), dma((LINE,)),
            ],
            compiler_params=pltpu.CompilerParams(
                collective_id=0, has_side_effects=True, vmem_limit_bytes=56 * 1024 * 1024
            ),
            cost_estimate=pl.CostEstimate(flops=flops, bytes_accessed=1 << 21, transcendentals=rows * WIN * tok),
            name="packed_attention",
        )(lengths, queries, keys, values, out_grad)

    return jax.shard_map(
        on_device,
        mesh=mesh,
        in_specs=(P("ctx", "head"), P("ctx", None), P("ctx", None), P("ctx", "head"), P()),
        out_specs=(P("ctx", "head"), P("ctx", "head"), P(("ctx", "head"), None), P(("ctx", "head"), None)),
        check_vma=False,
    )
```

```python
import functools
import math

import jax
import jax.numpy as jnp
from jax import lax
from jax.experimental import pallas as pl
from jax.experimental.pallas import tpu as pltpu
from jax.sharding import PartitionSpec as P

MESH = pl.DeviceIdType.MESH
WIN = 8
LINE = 4
CHUNKS = 2
NEG = -1e30


def dot_nn(a, b):
    return lax.dot_general(a, b, (((1,), (0,)), ((), ())), preferred_element_type=jnp.float32)


def dot_nt(a, b):
    return lax.dot_general(a, b, (((1,), (1,)), ((), ())), preferred_element_type=jnp.float32)


def kernel(
    shards, docs, len_ref, q_hbm, k_hbm, v_hbm, g_hbm,
    att_ref, dq_ref, dk_ref, dv_ref,
    fetch_sem, q_ref, g_ref, win, p_buf, ds_buf, s_buf, m_buf, m_now, l_now, acc, q_ext, g_ext, qt, gt,
    kept, mine, sib_out, sib_in, out_buf, relay_in, back_in,
    a_send, a_recv, relay_send, fwd_send, fwd_recv, sum_send, sum_recv,
    back_send, back_recv, col_send, col_recv, line_send, line_recv,
):
    me = lax.axis_index("ctx")
    core = lax.axis_index("head")
    tok, width = k_hbm.shape
    heads = q_hbm.shape[1] // width
    half = tok // 2
    scale = 1.0 / math.sqrt(width)
    scale2 = scale * math.log2(math.e)
    line = me // LINE
    place = me % LINE
    my_rows = pl.ds(pl.multiple_of(core * half, half), half)
    sib_rows = pl.ds(pl.multiple_of((1 - core) * half, half), half)
    quarter = half // CHUNKS

    def chunk_rows(whose, chunk):
        return pl.ds(pl.multiple_of(whose * half + chunk * quarter, quarter), quarter)
    sibling = (me, 1 - core)

    def remote(src, dst, send, recv, device):
        return pltpu.make_async_remote_copy(
            src_ref=src, dst_ref=dst, send_sem=send, recv_sem=recv, device_id=device, device_id_type=MESH
        )

    def ahead(step):
        return me + step + LINE * ((place + step) // LINE)

    def behind(step):
        return me - step - LINE * ((LINE - 1 - place + step) // LINE)

    def on_line(step):
        return line * LINE + (place + step + LINE) % LINE

    def distance(slot):
        step = slot % LINE
        wrap = (LINE - 1 - place + step) // LINE
        late = slot // LINE
        return step + LINE * (wrap + late - 2 * wrap * late)

    def exists(slot):
        return me - distance(slot) >= 0

    has_next = me + LINE < shards
    has_prev = line >= 1

    fetches = [
        pltpu.make_async_copy(source, target, fetch_sem.at[index])
        for index, (source, target) in enumerate(
            (
                (k_hbm, win.at[0, :, pl.ds(0, width)]),
                (v_hbm, win.at[0, :, pl.ds(width, width)]),
                (q_hbm, q_ref),
                (g_hbm, g_ref),
            )
        )
    ]
    for fetch in fetches:
        fetch.start()

    @pl.when(line < 2)
    def _():
        for slot in range(1, WIN):
            win[slot] = jnp.zeros(win.shape[1:], win.dtype)

    barrier = pltpu.get_barrier_semaphore()

    def greet(device):
        pl.semaphore_signal(barrier, inc=1, device_id=device, device_id_type=MESH)

    greet(sibling)
    for step in range(1, LINE):
        greet((on_line(step), core))
    for step in range(1, LINE):
        up, down = ahead(step), behind(step)
        far_up = jnp.logical_and(place + step >= LINE, up < shards)
        far_down = jnp.logical_and(place < step, down >= 0)

        @pl.when(far_up)
        def _():
            greet((up, core))

        @pl.when(far_down)
        def _():
            greet((down, core))


    @pl.when(has_next)
    def _():
        greet((me + LINE, core))

    @pl.when(has_prev)
    def _():
        greet((me - LINE, core))

    lines = shards // LINE
    near = (line + lines - 1) // lines + 1 - (line + 1) // lines
    far = place * (1 - (line + 2) // lines) + (LINE - 1 - place) * ((line + lines - 2) // lines)
    pl.semaphore_wait(barrier, LINE + near + far)
    fetches[0].wait()
    fetches[1].wait()

    def block_send(slot, device, chunk):
        rows = chunk_rows(core, chunk)
        return remote(
            win.at[0, rows], win.at[slot, rows], a_send.at[slot, chunk], a_recv.at[slot, chunk], (device, core)
        )

    def relay_copy(step, chunk):
        rows = chunk_rows(core, chunk)
        return remote(
            win.at[LINE, rows], win.at[LINE + step, rows],
            relay_send.at[step, chunk], a_recv.at[LINE + step, chunk], (on_line(step), core),
        )

    @pl.when(has_next)
    def _():
        for chunk in range(CHUNKS):
            block_send(LINE, me + LINE, chunk).start()

    for step in range(1, LINE):

        @pl.when(ahead(step) < shards)
        def _():
            for chunk in range(CHUNKS):
                block_send(step, ahead(step), chunk).start()

    lane = lax.broadcasted_iota(jnp.int32, (tok, width), 1)
    sub = lax.broadcasted_iota(jnp.int32, (tok, width), 0)

    def one_doc(doc, state):
        first, starts, ends = state
        here = lane[0:8] == doc
        last = first + len_ref[doc]
        return last, jnp.where(here, first, starts), jnp.where(here, last, ends)

    zero = jnp.zeros((8, width), jnp.int32)
    _, starts, ends = lax.fori_loop(0, docs, one_doc, (jnp.int32(0), zero, zero))
    starts, ends = starts[0:1], ends[0:1]
    row_pos = me * tok + sub
    inside = jnp.logical_and(row_pos >= starts, row_pos < ends)
    marks = jnp.where(inside, NEG, 0.0).astype(jnp.bfloat16)
    fetches[2].wait()
    fetches[3].wait()
    for h in range(heads):
        q_ext[h, :, 0:width] = q_ref[:, h * width : (h + 1) * width]
        q_ext[h, :, width:] = marks
    acc[...] = jnp.zeros(acc.shape, jnp.float32)
    m_now[...] = jnp.full(m_now.shape, NEG, jnp.float32)
    ones = jnp.ones((tok, width), jnp.bfloat16)

    def wide(x):
        return jnp.concatenate([x] * (tok // width), axis=1)

    def score_pass(slot, own):
        early = ((me - distance(slot)) * tok + sub) < starts
        keys = jnp.concatenate([win[slot, :, 0:width], early.astype(jnp.bfloat16)], axis=1)
        vals = jnp.concatenate([win[slot, :, width:], ones], axis=1)
        for h in range(heads):
            rows = slice(h * tok, (h + 1) * tok)
            scores = dot_nt(q_ext[h], keys)
            if own:
                col = lax.broadcasted_iota(jnp.int32, scores.shape, 1)
                row = lax.broadcasted_iota(jnp.int32, scores.shape, 0)
                scores = jnp.where(col <= row, scores, NEG)
            s_buf[h] = scores
            peak = jnp.max(scores, axis=1, keepdims=True) * scale2
            m_buf[slot, rows, :] = jnp.maximum(m_now[rows, :], peak)
        for h in range(heads):
            rows = slice(h * tok, (h + 1) * tok)
            new = m_buf[slot, rows, :]
            shrink = jnp.exp2(m_now[rows, :] - new)
            m_now[rows, :] = new
            low = jnp.exp2(s_buf[h] * scale2 - wide(new)).astype(jnp.bfloat16)
            p_buf[slot, rows, :] = low
            part = dot_nn(low, vals)
            acc[rows, 0:width] = acc[rows, 0:width] * shrink + part[:, 0:width]
            acc[rows, width:] = acc[rows, width:] * shrink + part[:, width:]

    score_pass(0, True)
    for h in range(heads):
        qt[:, h * tok : (h + 1) * tok] = q_ref[:, h * width : (h + 1) * width].T
        gt[:, h * tok : (h + 1) * tok] = g_ref[:, h * width : (h + 1) * width].T

    def cross_copy(slot, chunk):
        piece = win.at[slot, chunk_rows(core, chunk)]
        return remote(piece, piece, fwd_send.at[slot, chunk], fwd_recv.at[slot, chunk], sibling)

    def arrival(slot):
        @pl.when(exists(slot))
        def _():
            for chunk in range(CHUNKS):
                piece = win.at[slot, chunk_rows(core, chunk)]
                remote(piece, piece, fwd_send.at[slot, chunk], a_recv.at[slot, chunk], sibling).wait_recv()
                if slot == LINE:
                    for step in range(1, LINE):
                        relay_copy(step, chunk).start()
                cross_copy(slot, chunk).start()

    def arrival_end(slot):
        @pl.when(exists(slot))
        def _():
            for chunk in range(CHUNKS):
                piece = win.at[slot, chunk_rows(1 - core, chunk)]
                remote(piece, piece, fwd_send.at[slot, chunk], fwd_recv.at[slot, chunk], sibling).wait_recv()

    arrival(LINE)
    order = (4, 1, 2, 3, 5, 6, 7)
    for index, slot in enumerate(order):
        if index + 1 < len(order):
            arrival(order[index + 1])
        arrival_end(slot)
        score_pass(slot, False)

    for h in range(heads):
        rows = slice(h * tok, (h + 1) * tok)
        cols = slice(h * width, (h + 1) * width)
        inverse = 1.0 / acc[rows, width:]
        out = (acc[rows, 0:width] * inverse).astype(jnp.bfloat16)
        att_ref[:, cols] = out
        grads = g_ref[:, cols]
        total = -jnp.sum(grads.astype(jnp.float32) * out.astype(jnp.float32), axis=1, keepdims=True)
        high = total.astype(jnp.bfloat16).astype(jnp.float32)
        extra = jnp.where(lane == 0, high, jnp.where(lane == 1, total - high, 0.0))
        g_ext[h, :, 0:width] = grads
        g_ext[h, :, width:] = extra.astype(jnp.bfloat16)
        l_now[rows, :] = inverse

    def factor_pass(slot):
        vals = jnp.concatenate([win[slot, :, width:], ones], axis=1)
        for h in range(heads):
            rows = slice(h * tok, (h + 1) * tok)
            factor = jnp.exp2(m_buf[slot, rows, :] - m_now[rows, :]) * l_now[rows, :]
            probs = p_buf[slot, rows, :].astype(jnp.float32) * wide(factor)
            prob_grad = dot_nt(g_ext[h], vals)
            ds_buf[slot, rows, :] = (probs * prob_grad).astype(jnp.bfloat16)
            p_buf[slot, rows, :] = probs.astype(jnp.bfloat16)

    halves = (0, 1)

    def part_rows(part):
        return pl.ds(part * width, width)

    def sum_copy(slot, part):
        rows = part_rows(part)
        return remote(
            sib_out.at[slot, rows, sib_rows], sib_in.at[slot, rows], sum_send.at[slot, part], sum_recv.at[slot, part], sibling
        )

    def back_copy(step):
        return remote(
            out_buf.at[step], back_in.at[step], back_send.at[step], back_recv.at[step], (behind(step), core)
        )

    def line_copy(step, part):
        rows = part_rows(part)
        return remote(
            out_buf.at[LINE + step, rows], relay_in.at[step, rows],
            line_send.at[step, part], line_recv.at[step, part], (on_line(-step), core),
        )

    def col_copy(part):
        rows = part_rows(part)
        return remote(
            out_buf.at[LINE, rows], back_in.at[0, rows], col_send.at[part], col_recv.at[part], (me - LINE, core)
        )

    sides = ((1, gt, p_buf), (0, qt, ds_buf))

    def grad_pass(slot):
        for part, left, right in sides:
            total = dot_nn(left[...], right[slot])
            mine[slot, part_rows(part), :] = total
            sib_out[slot, part_rows(part), :] = total.astype(jnp.bfloat16)
            sum_copy(slot, part).start()

    def return_part(slot):
        for part, _, _ in sides:
            rows = part_rows(part)
            sum_copy(slot, part).wait_recv()
            total = mine[slot, rows, my_rows] + sib_in[slot, rows, :].astype(jnp.float32)
            if slot in (0, LINE):
                kept[slot // LINE, rows, :] = total
            else:
                out_buf[slot, rows, :] = total.astype(jnp.bfloat16)
            if slot > LINE:

                @pl.when(has_prev)
                def _():
                    line_copy(slot - LINE, part).start()

        if 0 < slot < LINE:

            @pl.when(exists(slot))
            def _():
                back_copy(slot).start()

    back_order = (6, 5, 7, 3, 2, 1, 4, 0)
    for index in range(WIN + 2):
        if 1 <= index <= WIN:
            grad_pass(back_order[index - 1])
        if index < WIN:
            factor_pass(back_order[index])
        if index >= 2:
            return_part(back_order[index - 2])

    @pl.when(has_prev)
    def _():
        for part, _, _ in sides:
            rows = part_rows(part)
            total = kept[1, rows, :]
            for step in range(1, LINE):
                line_copy(step, part).wait_recv()
                total = total + relay_in[step, rows, :].astype(jnp.float32)
            out_buf[LINE, rows, :] = total.astype(jnp.bfloat16)
            col_copy(part).start()

    for h in range(heads):
        rows = slice(h * tok, (h + 1) * tok)
        total = dot_nn(ds_buf[0, rows, :], win[0, :, 0:width])
        for slot in range(1, WIN):
            total = total + dot_nn(ds_buf[slot, rows, :], win[slot, :, 0:width])
        dq_ref[:, h * width : (h + 1) * width] = (total * scale).astype(jnp.bfloat16)

    for step in range(1, LINE):

        @pl.when(ahead(step) < shards)
        def _():
            back_copy(step).wait_recv()
            kept[0] = kept[0] + back_in[step].astype(jnp.float32)

    for part, _, _ in sides:
        rows = part_rows(part)

        @pl.when(has_next)
        def _():
            col_copy(part).wait_recv()
            kept[0, rows, :] = kept[0, rows, :] + back_in[0, rows, :].astype(jnp.float32)

        if part:
            dv_ref[...] = kept[0, rows, :].T.astype(jnp.bfloat16)
        else:
            dk_ref[...] = (kept[0, rows, :] * scale).T.astype(jnp.bfloat16)

    @pl.when(has_next)
    def _():
        for chunk in range(CHUNKS):
            block_send(LINE, me + LINE, chunk).wait_send()

    for step in range(1, LINE):

        @pl.when(ahead(step) < shards)
        def _():
            for chunk in range(CHUNKS):
                block_send(step, ahead(step), chunk).wait_send()

    @pl.when(has_prev)
    def _():
        for step in range(1, LINE):
            for chunk in range(CHUNKS):
                relay_copy(step, chunk).wait_send()
            for part in halves:
                line_copy(step, part).wait_send()
        for part in halves:
            col_copy(part).wait_send()

    for slot in range(1, WIN):

        @pl.when(exists(slot))
        def _():
            for chunk in range(CHUNKS):
                cross_copy(slot, chunk).wait_send()

    for slot in range(WIN):
        for part in halves:
            sum_copy(slot, part).wait_send()

    for step in range(1, LINE):

        @pl.when(behind(step) >= 0)
        def _():
            back_copy(step).wait_send()


def hand_on(*refs):
    for source, target in zip(refs[:4], refs[4:]):
        target[...] = source[...]


def solution(mesh):
    shards = mesh.shape["ctx"]

    def on_device(queries, keys, values, out_grad, lengths):
        tok, width = keys.shape
        heads = queries.shape[1] // width
        rows = heads * tok
        half = tok // 2
        bf16, f32 = jnp.bfloat16, jnp.float32
        vmem = pl.BlockSpec(memory_space=pltpu.VMEM)
        dma = pltpu.SemaphoreType.DMA
        flops = 6 * 2 * rows * WIN * tok * width
        results = pl.pallas_call(
            functools.partial(kernel, shards, lengths.shape[0]),
            out_shape=(
                jax.ShapeDtypeStruct(queries.shape, bf16),
                jax.ShapeDtypeStruct(queries.shape, bf16),
                jax.ShapeDtypeStruct((half, width), bf16),
                jax.ShapeDtypeStruct((half, width), bf16),
            ),
            in_specs=[pl.BlockSpec(memory_space=pltpu.SMEM)] + [pl.BlockSpec(memory_space=pl.ANY)] * 4,
            out_specs=(vmem,) * 4,
            scratch_shapes=[
                dma((4,)),
                pltpu.VMEM(queries.shape, bf16),
                pltpu.VMEM(queries.shape, bf16),
                pltpu.VMEM((WIN, tok, 2 * width), bf16),
                pltpu.VMEM((WIN, rows, tok), bf16),
                pltpu.VMEM((WIN, rows, tok), bf16),
                pltpu.VMEM((heads, tok, tok), f32),
                pltpu.VMEM((WIN, rows, width), f32),
                pltpu.VMEM((rows, width), f32),
                pltpu.VMEM((rows, width), f32),
                pltpu.VMEM((rows, 2 * width), f32),
                pltpu.VMEM((heads, tok, 2 * width), bf16),
                pltpu.VMEM((heads, tok, 2 * width), bf16),
                pltpu.VMEM((width, rows), bf16),
                pltpu.VMEM((width, rows), bf16),
                pltpu.VMEM((2, 2 * width, half), f32),
                pltpu.VMEM((WIN, 2 * width, tok), f32),
                pltpu.VMEM((WIN, 2 * width, tok), bf16),
                pltpu.VMEM((WIN, 2 * width, half), bf16),
                pltpu.VMEM((WIN, 2 * width, half), bf16),
                pltpu.VMEM((LINE, 2 * width, half), bf16),
                pltpu.VMEM((LINE, 2 * width, half), bf16),
                dma((WIN, CHUNKS)), dma((WIN, CHUNKS)), dma((LINE, CHUNKS)), dma((WIN, CHUNKS)), dma((WIN, CHUNKS)),
                dma((WIN, 2)), dma((WIN, 2)), dma((LINE,)), dma((LINE,)), dma((2,)), dma((2,)),
                dma((LINE, 2)), dma((LINE, 2)),
            ],
            compiler_params=pltpu.CompilerParams(
                collective_id=0, has_side_effects=True, vmem_limit_bytes=56 * 1024 * 1024
            ),
            cost_estimate=pl.CostEstimate(flops=flops, bytes_accessed=1 << 21, transcendentals=rows * WIN * tok),
            name="packed_attention",
        )(lengths, queries, keys, values, out_grad)
        return pl.pallas_call(
            hand_on,
            out_shape=tuple(jax.ShapeDtypeStruct(r.shape, r.dtype) for r in results),
            in_specs=[vmem] * 4,
            out_specs=(vmem,) * 4,
            name="hand_on",
        )(*results)

    return jax.shard_map(
        on_device,
        mesh=mesh,
        in_specs=(P("ctx", "head"), P("ctx", None), P("ctx", None), P("ctx", "head"), P()),
        out_specs=(P("ctx", "head"), P("ctx", "head"), P(("ctx", "head"), None), P(("ctx", "head"), None)),
        check_vma=False,
    )
```

```python
import functools
import math

import jax
import jax.numpy as jnp
from jax import lax
from jax.experimental import pallas as pl
from jax.experimental.pallas import tpu as pltpu
from jax.sharding import PartitionSpec as P

MESH = pl.DeviceIdType.MESH
WIN = 8
LINE = 4
CHUNKS = 2
NEG = -1e30


def dot_nn(a, b):
    return lax.dot_general(a, b, (((1,), (0,)), ((), ())), preferred_element_type=jnp.float32)


def dot_nt(a, b):
    return lax.dot_general(a, b, (((1,), (1,)), ((), ())), preferred_element_type=jnp.float32)


def kernel(
    shards, docs, len_ref, q_hbm, k_hbm, v_hbm, g_hbm,
    att_ref, dq_ref, dk_ref, dv_ref,
    fetch_sem, q_ref, g_ref, win, p_buf, ds_buf, s_buf, m_buf, m_now, l_now, acc, q_ext, g_ext, qt, gt,
    kept, mine, sib_out, sib_in, out_buf, relay_in, back_in,
    a_send, a_recv, relay_send, fwd_send, fwd_recv, sum_send, sum_recv,
    back_send, back_recv, col_send, col_recv, line_send, line_recv,
):
    me = lax.axis_index("ctx")
    core = lax.axis_index("head")
    tok, width = k_hbm.shape
    heads = q_hbm.shape[1] // width
    half = tok // 2
    scale = 1.0 / math.sqrt(width)
    scale2 = scale * math.log2(math.e)
    line = me // LINE
    place = me % LINE
    my_rows = pl.ds(pl.multiple_of(core * half, half), half)
    sib_rows = pl.ds(pl.multiple_of((1 - core) * half, half), half)
    quarter = half // CHUNKS

    def chunk_rows(whose, chunk):
        return pl.ds(pl.multiple_of(whose * half + chunk * quarter, quarter), quarter)
    sibling = (me, 1 - core)

    def remote(src, dst, send, recv, device):
        return pltpu.make_async_remote_copy(
            src_ref=src, dst_ref=dst, send_sem=send, recv_sem=recv, device_id=device, device_id_type=MESH
        )

    def ahead(step):
        return me + step + LINE * ((place + step) // LINE)

    def behind(step):
        return me - step - LINE * ((LINE - 1 - place + step) // LINE)

    def on_line(step):
        return line * LINE + (place + step + LINE) % LINE

    def distance(slot):
        step = slot % LINE
        wrap = (LINE - 1 - place + step) // LINE
        late = slot // LINE
        return step + LINE * (wrap + late - 2 * wrap * late)

    def exists(slot):
        return me - distance(slot) >= 0

    has_next = me + LINE < shards
    has_prev = line >= 1

    fetches = [
        pltpu.make_async_copy(source, target, fetch_sem.at[index])
        for index, (source, target) in enumerate(
            (
                (k_hbm, win.at[0, :, pl.ds(0, width)]),
                (v_hbm, win.at[0, :, pl.ds(width, width)]),
                (q_hbm, q_ref),
                (g_hbm, g_ref),
            )
        )
    ]
    for fetch in fetches:
        fetch.start()

    @pl.when(line < 2)
    def _():
        for slot in range(1, WIN):
            win[slot] = jnp.zeros(win.shape[1:], win.dtype)

    barrier = pltpu.get_barrier_semaphore()

    def greet(device):
        pl.semaphore_signal(barrier, inc=1, device_id=device, device_id_type=MESH)

    greet(sibling)
    for step in range(1, LINE):
        greet((on_line(step), core))
    for step in range(1, LINE):
        up, down = ahead(step), behind(step)
        far_up = jnp.logical_and(place + step >= LINE, up < shards)
        far_down = jnp.logical_and(place < step, down >= 0)

        @pl.when(far_up)
        def _():
            greet((up, core))

        @pl.when(far_down)
        def _():
            greet((down, core))


    @pl.when(has_next)
    def _():
        greet((me + LINE, core))

    @pl.when(has_prev)
    def _():
        greet((me - LINE, core))

    lines = shards // LINE
    near = (line + lines - 1) // lines + 1 - (line + 1) // lines
    far = place * (1 - (line + 2) // lines) + (LINE - 1 - place) * ((line + lines - 2) // lines)
    pl.semaphore_wait(barrier, LINE + near + far)
    fetches[0].wait()
    fetches[1].wait()

    def block_send(slot, device, chunk):
        rows = chunk_rows(core, chunk)
        return remote(
            win.at[0, rows], win.at[slot, rows], a_send.at[slot, chunk], a_recv.at[slot, chunk], (device, core)
        )

    def relay_copy(step, chunk):
        rows = chunk_rows(core, chunk)
        return remote(
            win.at[LINE, rows], win.at[LINE + step, rows],
            relay_send.at[step, chunk], a_recv.at[LINE + step, chunk], (on_line(step), core),
        )

    @pl.when(has_next)
    def _():
        for chunk in range(CHUNKS):
            block_send(LINE, me + LINE, chunk).start()

    for step in range(1, LINE):

        @pl.when(ahead(step) < shards)
        def _():
            for chunk in range(CHUNKS):
                block_send(step, ahead(step), chunk).start()

    lane = lax.broadcasted_iota(jnp.int32, (tok, width), 1)
    sub = lax.broadcasted_iota(jnp.int32, (tok, width), 0)

    def one_doc(doc, state):
        first, starts, ends = state
        here = lane[0:8] == doc
        last = first + len_ref[doc]
        return last, jnp.where(here, first, starts), jnp.where(here, last, ends)

    zero = jnp.zeros((8, width), jnp.int32)
    _, starts, ends = lax.fori_loop(0, docs, one_doc, (jnp.int32(0), zero, zero))
    starts, ends = starts[0:1], ends[0:1]
    row_pos = me * tok + sub
    inside = jnp.logical_and(row_pos >= starts, row_pos < ends)
    marks = jnp.where(inside, NEG, 0.0).astype(jnp.bfloat16)
    fetches[2].wait()
    fetches[3].wait()
    for h in range(heads):
        q_ext[h, :, 0:width] = q_ref[:, h * width : (h + 1) * width]
        q_ext[h, :, width:] = marks
    acc[...] = jnp.zeros(acc.shape, jnp.float32)
    m_now[...] = jnp.full(m_now.shape, NEG, jnp.float32)
    ones = jnp.ones((tok, width), jnp.bfloat16)

    def wide(x):
        return jnp.concatenate([x] * (tok // width), axis=1)

    def score_pass(slot, own):
        early = ((me - distance(slot)) * tok + sub) < starts
        keys = jnp.concatenate([win[slot, :, 0:width], early.astype(jnp.bfloat16)], axis=1)
        vals = jnp.concatenate([win[slot, :, width:], ones], axis=1)
        for h in range(heads):
            rows = slice(h * tok, (h + 1) * tok)
            scores = dot_nt(q_ext[h], keys)
            if own:
                col = lax.broadcasted_iota(jnp.int32, scores.shape, 1)
                row = lax.broadcasted_iota(jnp.int32, scores.shape, 0)
                scores = jnp.where(col <= row, scores, NEG)
            s_buf[h] = scores
            peak = jnp.max(scores, axis=1, keepdims=True) * scale2
            m_buf[slot, rows, :] = jnp.maximum(m_now[rows, :], peak)
        for h in range(heads):
            rows = slice(h * tok, (h + 1) * tok)
            new = m_buf[slot, rows, :]
            shrink = jnp.exp2(m_now[rows, :] - new)
            m_now[rows, :] = new
            low = jnp.exp2(s_buf[h] * scale2 - wide(new)).astype(jnp.bfloat16)
            p_buf[slot, rows, :] = low
            part = dot_nn(low, vals)
            acc[rows, 0:width] = acc[rows, 0:width] * shrink + part[:, 0:width]
            acc[rows, width:] = acc[rows, width:] * shrink + part[:, width:]

    score_pass(0, True)
    for h in range(heads):
        qt[:, h * tok : (h + 1) * tok] = q_ref[:, h * width : (h + 1) * width].T
        gt[:, h * tok : (h + 1) * tok] = g_ref[:, h * width : (h + 1) * width].T

    def cross_copy(slot, chunk):
        piece = win.at[slot, chunk_rows(core, chunk)]
        return remote(piece, piece, fwd_send.at[slot, chunk], fwd_recv.at[slot, chunk], sibling)

    def arrival(slot):
        @pl.when(exists(slot))
        def _():
            for chunk in range(CHUNKS):
                piece = win.at[slot, chunk_rows(core, chunk)]
                remote(piece, piece, fwd_send.at[slot, chunk], a_recv.at[slot, chunk], sibling).wait_recv()
                if slot == LINE:
                    for step in range(1, LINE):
                        relay_copy(step, chunk).start()
                cross_copy(slot, chunk).start()

    def arrival_end(slot):
        @pl.when(exists(slot))
        def _():
            for chunk in range(CHUNKS):
                piece = win.at[slot, chunk_rows(1 - core, chunk)]
                remote(piece, piece, fwd_send.at[slot, chunk], fwd_recv.at[slot, chunk], sibling).wait_recv()

    arrival(LINE)
    order = (4, 1, 2, 3, 5, 6, 7)
    for index, slot in enumerate(order):
        if index + 1 < len(order):
            arrival(order[index + 1])
        arrival_end(slot)
        score_pass(slot, False)

    for h in range(heads):
        rows = slice(h * tok, (h + 1) * tok)
        cols = slice(h * width, (h + 1) * width)
        inverse = 1.0 / acc[rows, width:]
        out = (acc[rows, 0:width] * inverse).astype(jnp.bfloat16)
        att_ref[:, cols] = out
        grads = g_ref[:, cols]
        terms = grads.astype(jnp.float32) * out.astype(jnp.float32)
        coarse = terms.astype(jnp.bfloat16)
        fine = (terms - coarse.astype(jnp.float32)).astype(jnp.bfloat16)
        total = -dot_nn(jnp.concatenate([coarse, fine], axis=1), jnp.ones((2 * width, width), jnp.bfloat16))
        high = total.astype(jnp.bfloat16).astype(jnp.float32)
        extra = jnp.where(lane == 0, high, jnp.where(lane == 1, total - high, 0.0))
        g_ext[h, :, 0:width] = grads
        g_ext[h, :, width:] = extra.astype(jnp.bfloat16)
        l_now[rows, :] = inverse

    def factor_pass(slot):
        vals = jnp.concatenate([win[slot, :, width:], ones], axis=1)
        for h in range(heads):
            rows = slice(h * tok, (h + 1) * tok)
            factor = jnp.exp2(m_buf[slot, rows, :] - m_now[rows, :]) * l_now[rows, :]
            probs = p_buf[slot, rows, :].astype(jnp.float32) * wide(factor)
            prob_grad = dot_nt(g_ext[h], vals)
            ds_buf[slot, rows, :] = (probs * prob_grad).astype(jnp.bfloat16)
            p_buf[slot, rows, :] = probs.astype(jnp.bfloat16)

    halves = (0, 1)

    def part_rows(part):
        return pl.ds(part * width, width)

    def sum_copy(slot, part):
        rows = part_rows(part)
        return remote(
            sib_out.at[slot, rows, sib_rows], sib_in.at[slot, rows], sum_send.at[slot, part], sum_recv.at[slot, part], sibling
        )

    def back_copy(step):
        return remote(
            out_buf.at[step], back_in.at[step], back_send.at[step], back_recv.at[step], (behind(step), core)
        )

    def line_copy(step, part):
        rows = part_rows(part)
        return remote(
            out_buf.at[LINE + step, rows], relay_in.at[step, rows],
            line_send.at[step, part], line_recv.at[step, part], (on_line(-step), core),
        )

    def col_copy(part):
        rows = part_rows(part)
        return remote(
            out_buf.at[LINE, rows], back_in.at[0, rows], col_send.at[part], col_recv.at[part], (me - LINE, core)
        )

    sides = ((1, gt, p_buf), (0, qt, ds_buf))

    def grad_pass(slot):
        for part, left, right in sides:
            total = dot_nn(left[...], right[slot])
            mine[slot, part_rows(part), :] = total
            sib_out[slot, part_rows(part), :] = total.astype(jnp.bfloat16)
            sum_copy(slot, part).start()

    def return_part(slot):
        for part, _, _ in sides:
            rows = part_rows(part)
            sum_copy(slot, part).wait_recv()
            total = mine[slot, rows, my_rows] + sib_in[slot, rows, :].astype(jnp.float32)
            if slot in (0, LINE):
                kept[slot // LINE, rows, :] = total
            else:
                out_buf[slot, rows, :] = total.astype(jnp.bfloat16)
            if slot > LINE:

                @pl.when(has_prev)
                def _():
                    line_copy(slot - LINE, part).start()

        if 0 < slot < LINE:

            @pl.when(exists(slot))
            def _():
                back_copy(slot).start()

    back_order = (6, 5, 7, 3, 2, 1, 4, 0)
    for index in range(WIN + 2):
        if 1 <= index <= WIN:
            grad_pass(back_order[index - 1])
        if index >= 2:
            return_part(back_order[index - 2])
        if index < WIN:
            factor_pass(back_order[index])

    @pl.when(has_prev)
    def _():
        for part, _, _ in sides:
            rows = part_rows(part)
            total = kept[1, rows, :]
            for step in range(1, LINE):
                line_copy(step, part).wait_recv()
                total = total + relay_in[step, rows, :].astype(jnp.float32)
            out_buf[LINE, rows, :] = total.astype(jnp.bfloat16)
            col_copy(part).start()

    for h in range(heads):
        rows = slice(h * tok, (h + 1) * tok)
        total = dot_nn(ds_buf[0, rows, :], win[0, :, 0:width])
        for slot in range(1, WIN):
            total = total + dot_nn(ds_buf[slot, rows, :], win[slot, :, 0:width])
        dq_ref[:, h * width : (h + 1) * width] = (total * scale).astype(jnp.bfloat16)

    for step in range(1, LINE):

        @pl.when(ahead(step) < shards)
        def _():
            back_copy(step).wait_recv()
            kept[0] = kept[0] + back_in[step].astype(jnp.float32)

    for part, _, _ in sides:
        rows = part_rows(part)

        @pl.when(has_next)
        def _():
            col_copy(part).wait_recv()
            kept[0, rows, :] = kept[0, rows, :] + back_in[0, rows, :].astype(jnp.float32)

        if part:
            dv_ref[...] = kept[0, rows, :].T.astype(jnp.bfloat16)
        else:
            dk_ref[...] = (kept[0, rows, :] * scale).T.astype(jnp.bfloat16)

    @pl.when(has_next)
    def _():
        for chunk in range(CHUNKS):
            block_send(LINE, me + LINE, chunk).wait_send()

    for step in range(1, LINE):

        @pl.when(ahead(step) < shards)
        def _():
            for chunk in range(CHUNKS):
                block_send(step, ahead(step), chunk).wait_send()

    @pl.when(has_prev)
    def _():
        for step in range(1, LINE):
            for chunk in range(CHUNKS):
                relay_copy(step, chunk).wait_send()
            for part in halves:
                line_copy(step, part).wait_send()
        for part in halves:
            col_copy(part).wait_send()

    for slot in range(1, WIN):

        @pl.when(exists(slot))
        def _():
            for chunk in range(CHUNKS):
                cross_copy(slot, chunk).wait_send()

    for slot in range(WIN):
        for part in halves:
            sum_copy(slot, part).wait_send()

    for step in range(1, LINE):

        @pl.when(behind(step) >= 0)
        def _():
            back_copy(step).wait_send()


def hand_on(*refs):
    for source, target in zip(refs[:4], refs[4:]):
        target[...] = source[...]


def solution(mesh):
    shards = mesh.shape["ctx"]

    def on_device(queries, keys, values, out_grad, lengths):
        tok, width = keys.shape
        heads = queries.shape[1] // width
        rows = heads * tok
        half = tok // 2
        bf16, f32 = jnp.bfloat16, jnp.float32
        vmem = pl.BlockSpec(memory_space=pltpu.VMEM)
        dma = pltpu.SemaphoreType.DMA
        flops = 6 * 2 * rows * WIN * tok * width
        results = pl.pallas_call(
            functools.partial(kernel, shards, lengths.shape[0]),
            out_shape=(
                jax.ShapeDtypeStruct(queries.shape, bf16),
                jax.ShapeDtypeStruct(queries.shape, bf16),
                jax.ShapeDtypeStruct((half, width), bf16),
                jax.ShapeDtypeStruct((half, width), bf16),
            ),
            in_specs=[pl.BlockSpec(memory_space=pltpu.SMEM)] + [pl.BlockSpec(memory_space=pl.ANY)] * 4,
            out_specs=(vmem,) * 4,
            scratch_shapes=[
                dma((4,)),
                pltpu.VMEM(queries.shape, bf16),
                pltpu.VMEM(queries.shape, bf16),
                pltpu.VMEM((WIN, tok, 2 * width), bf16),
                pltpu.VMEM((WIN, rows, tok), bf16),
                pltpu.VMEM((WIN, rows, tok), bf16),
                pltpu.VMEM((heads, tok, tok), f32),
                pltpu.VMEM((WIN, rows, width), f32),
                pltpu.VMEM((rows, width), f32),
                pltpu.VMEM((rows, width), f32),
                pltpu.VMEM((rows, 2 * width), f32),
                pltpu.VMEM((heads, tok, 2 * width), bf16),
                pltpu.VMEM((heads, tok, 2 * width), bf16),
                pltpu.VMEM((width, rows), bf16),
                pltpu.VMEM((width, rows), bf16),
                pltpu.VMEM((2, 2 * width, half), f32),
                pltpu.VMEM((WIN, 2 * width, tok), f32),
                pltpu.VMEM((WIN, 2 * width, tok), bf16),
                pltpu.VMEM((WIN, 2 * width, half), bf16),
                pltpu.VMEM((WIN, 2 * width, half), bf16),
                pltpu.VMEM((LINE, 2 * width, half), bf16),
                pltpu.VMEM((LINE, 2 * width, half), bf16),
                dma((WIN, CHUNKS)), dma((WIN, CHUNKS)), dma((LINE, CHUNKS)), dma((WIN, CHUNKS)), dma((WIN, CHUNKS)),
                dma((WIN, 2)), dma((WIN, 2)), dma((LINE,)), dma((LINE,)), dma((2,)), dma((2,)),
                dma((LINE, 2)), dma((LINE, 2)),
            ],
            compiler_params=pltpu.CompilerParams(
                collective_id=0, has_side_effects=True, vmem_limit_bytes=56 * 1024 * 1024
            ),
            cost_estimate=pl.CostEstimate(flops=flops, bytes_accessed=1 << 21, transcendentals=rows * WIN * tok),
            name="packed_attention",
        )(lengths, queries, keys, values, out_grad)
        return pl.pallas_call(
            hand_on,
            out_shape=tuple(jax.ShapeDtypeStruct(r.shape, r.dtype) for r in results),
            in_specs=[vmem] * 4,
            out_specs=(vmem,) * 4,
            name="hand_on",
        )(*results)

    return jax.shard_map(
        on_device,
        mesh=mesh,
        in_specs=(P("ctx", "head"), P("ctx", None), P("ctx", None), P("ctx", "head"), P()),
        out_specs=(P("ctx", "head"), P("ctx", "head"), P(("ctx", "head"), None), P(("ctx", "head"), None)),
        check_vma=False,
    )
```

```python
import functools
import math

import jax
import jax.numpy as jnp
from jax import lax
from jax.experimental import pallas as pl
from jax.experimental.pallas import tpu as pltpu
from jax.sharding import PartitionSpec as P

MESH = pl.DeviceIdType.MESH
WIN = 8
LINE = 4
CHUNKS = 2
NEG = -1e30


def dot_nn(a, b):
    return lax.dot_general(a, b, (((1,), (0,)), ((), ())), preferred_element_type=jnp.float32)


def dot_nt(a, b):
    return lax.dot_general(a, b, (((1,), (1,)), ((), ())), preferred_element_type=jnp.float32)


def kernel(
    shards, docs, len_ref, q_hbm, k_hbm, v_hbm, g_hbm,
    att_ref, dq_ref, dk_ref, dv_ref,
    fetch_sem, q_ref, g_ref, win, p_buf, ds_buf, s_buf, m_buf, m_now, l_now, acc, q_ext, g_ext, qt, gt,
    kept, mine, sib_out, sib_in, out_buf, relay_in, back_in,
    a_send, a_recv, relay_send, fwd_send, fwd_recv, sum_send, sum_recv,
    back_send, back_recv, col_send, col_recv, line_send, line_recv,
):
    me = lax.axis_index("ctx")
    core = lax.axis_index("head")
    tok, width = k_hbm.shape
    heads = q_hbm.shape[1] // width
    half = tok // 2
    scale = 1.0 / math.sqrt(width)
    scale2 = scale * math.log2(math.e)
    line = me // LINE
    place = me % LINE
    my_rows = pl.ds(pl.multiple_of(core * half, half), half)
    sib_rows = pl.ds(pl.multiple_of((1 - core) * half, half), half)
    quarter = half // CHUNKS

    def chunk_rows(whose, chunk):
        return pl.ds(pl.multiple_of(whose * half + chunk * quarter, quarter), quarter)
    sibling = (me, 1 - core)

    def remote(src, dst, send, recv, device):
        return pltpu.make_async_remote_copy(
            src_ref=src, dst_ref=dst, send_sem=send, recv_sem=recv, device_id=device, device_id_type=MESH
        )

    def ahead(step):
        return me + step + LINE * ((place + step) // LINE)

    def behind(step):
        return me - step - LINE * ((LINE - 1 - place + step) // LINE)

    def on_line(step):
        return line * LINE + (place + step + LINE) % LINE

    def distance(slot):
        step = slot % LINE
        wrap = (LINE - 1 - place + step) // LINE
        late = slot // LINE
        return step + LINE * (wrap + late - 2 * wrap * late)

    def exists(slot):
        return me - distance(slot) >= 0

    has_next = me + LINE < shards
    has_prev = line >= 1

    fetches = [
        pltpu.make_async_copy(source, target, fetch_sem.at[index])
        for index, (source, target) in enumerate(
            (
                (k_hbm, win.at[0, :, pl.ds(0, width)]),
                (v_hbm, win.at[0, :, pl.ds(width, width)]),
                (q_hbm, q_ref),
                (g_hbm, g_ref),
            )
        )
    ]
    for fetch in fetches:
        fetch.start()

    @pl.when(line < 2)
    def _():
        for slot in range(1, WIN):
            win[slot] = jnp.zeros(win.shape[1:], win.dtype)

    barrier = pltpu.get_barrier_semaphore()

    def greet(device):
        pl.semaphore_signal(barrier, inc=1, device_id=device, device_id_type=MESH)

    greet(sibling)
    for step in range(1, LINE):
        greet((on_line(step), core))
    for step in range(1, LINE):
        up, down = ahead(step), behind(step)
        far_up = jnp.logical_and(place + step >= LINE, up < shards)
        far_down = jnp.logical_and(place < step, down >= 0)

        @pl.when(far_up)
        def _():
            greet((up, core))

        @pl.when(far_down)
        def _():
            greet((down, core))


    @pl.when(has_next)
    def _():
        greet((me + LINE, core))

    @pl.when(has_prev)
    def _():
        greet((me - LINE, core))

    lines = shards // LINE
    near = (line + lines - 1) // lines + 1 - (line + 1) // lines
    far = place * (1 - (line + 2) // lines) + (LINE - 1 - place) * ((line + lines - 2) // lines)
    pl.semaphore_wait(barrier, LINE + near + far)
    fetches[0].wait()
    fetches[1].wait()

    def block_send(slot, device, chunk):
        rows = chunk_rows(core, chunk)
        return remote(
            win.at[0, rows], win.at[slot, rows], a_send.at[slot, chunk], a_recv.at[slot, chunk], (device, core)
        )

    def relay_copy(step, chunk):
        rows = chunk_rows(core, chunk)
        return remote(
            win.at[LINE, rows], win.at[LINE + step, rows],
            relay_send.at[step, chunk], a_recv.at[LINE + step, chunk], (on_line(step), core),
        )

    @pl.when(has_next)
    def _():
        for chunk in range(CHUNKS):
            block_send(LINE, me + LINE, chunk).start()

    for step in range(1, LINE):

        @pl.when(place + step < LINE)
        def _():
            for chunk in range(CHUNKS):
                block_send(step, ahead(step), chunk).start()

    lane = lax.broadcasted_iota(jnp.int32, (tok, width), 1)
    sub = lax.broadcasted_iota(jnp.int32, (tok, width), 0)

    def one_doc(doc, state):
        first, starts, ends = state
        here = lane[0:8] == doc
        last = first + len_ref[doc]
        return last, jnp.where(here, first, starts), jnp.where(here, last, ends)

    zero = jnp.zeros((8, width), jnp.int32)
    _, starts, ends = lax.fori_loop(0, docs, one_doc, (jnp.int32(0), zero, zero))
    starts, ends = starts[0:1], ends[0:1]
    row_pos = me * tok + sub
    inside = jnp.logical_and(row_pos >= starts, row_pos < ends)
    marks = jnp.where(inside, NEG, 0.0).astype(jnp.bfloat16)
    fetches[2].wait()
    fetches[3].wait()
    for h in range(heads):
        q_ext[h, :, 0:width] = q_ref[:, h * width : (h + 1) * width]
        q_ext[h, :, width:] = marks
    acc[...] = jnp.zeros(acc.shape, jnp.float32)
    m_now[...] = jnp.full(m_now.shape, NEG, jnp.float32)
    ones = jnp.ones((tok, width), jnp.bfloat16)

    def wide(x):
        return jnp.concatenate([x] * (tok // width), axis=1)

    def score_pass(slot, own):
        early = ((me - distance(slot)) * tok + sub) < starts
        keys = jnp.concatenate([win[slot, :, 0:width], early.astype(jnp.bfloat16)], axis=1)
        vals = jnp.concatenate([win[slot, :, width:], ones], axis=1)
        for h in range(heads):
            rows = slice(h * tok, (h + 1) * tok)
            scores = dot_nt(q_ext[h], keys)
            if own:
                col = lax.broadcasted_iota(jnp.int32, scores.shape, 1)
                row = lax.broadcasted_iota(jnp.int32, scores.shape, 0)
                scores = jnp.where(col <= row, scores, NEG)
            s_buf[h] = scores
            peak = jnp.max(scores, axis=1, keepdims=True) * scale2
            m_buf[slot, rows, :] = jnp.maximum(m_now[rows, :], peak)
        for h in range(heads):
            rows = slice(h * tok, (h + 1) * tok)
            new = m_buf[slot, rows, :]
            shrink = jnp.exp2(m_now[rows, :] - new)
            m_now[rows, :] = new
            low = jnp.exp2(s_buf[h] * scale2 - wide(new)).astype(jnp.bfloat16)
            p_buf[slot, rows, :] = low
            part = dot_nn(low, vals)
            acc[rows, 0:width] = acc[rows, 0:width] * shrink + part[:, 0:width]
            acc[rows, width:] = acc[rows, width:] * shrink + part[:, width:]

    for step in range(1, LINE):

        @pl.when(jnp.logical_and(place + step >= LINE, ahead(step) < shards))
        def _():
            for chunk in range(CHUNKS):
                block_send(step, ahead(step), chunk).start()

    score_pass(0, True)
    for h in range(heads):
        qt[:, h * tok : (h + 1) * tok] = q_ref[:, h * width : (h + 1) * width].T
        gt[:, h * tok : (h + 1) * tok] = g_ref[:, h * width : (h + 1) * width].T

    def cross_copy(slot, chunk):
        piece = win.at[slot, chunk_rows(core, chunk)]
        return remote(piece, piece, fwd_send.at[slot, chunk], fwd_recv.at[slot, chunk], sibling)

    def arrival(slot):
        @pl.when(exists(slot))
        def _():
            for chunk in range(CHUNKS):
                piece = win.at[slot, chunk_rows(core, chunk)]
                remote(piece, piece, fwd_send.at[slot, chunk], a_recv.at[slot, chunk], sibling).wait_recv()
                if slot == LINE:
                    for step in range(1, LINE):
                        relay_copy(step, chunk).start()
                cross_copy(slot, chunk).start()

    def arrival_end(slot):
        @pl.when(exists(slot))
        def _():
            for chunk in range(CHUNKS):
                piece = win.at[slot, chunk_rows(1 - core, chunk)]
                remote(piece, piece, fwd_send.at[slot, chunk], fwd_recv.at[slot, chunk], sibling).wait_recv()

    arrival(LINE)
    order = (4, 1, 2, 3, 5, 6, 7)
    for index, slot in enumerate(order):
        if index + 1 < len(order):
            arrival(order[index + 1])
        arrival_end(slot)
        score_pass(slot, False)

    for h in range(heads):
        rows = slice(h * tok, (h + 1) * tok)
        cols = slice(h * width, (h + 1) * width)
        inverse = 1.0 / acc[rows, width:]
        out = (acc[rows, 0:width] * inverse).astype(jnp.bfloat16)
        att_ref[:, cols] = out
        grads = g_ref[:, cols]
        terms = grads.astype(jnp.float32) * out.astype(jnp.float32)
        coarse = terms.astype(jnp.bfloat16)
        fine = (terms - coarse.astype(jnp.float32)).astype(jnp.bfloat16)
        total = -dot_nn(jnp.concatenate([coarse, fine], axis=1), jnp.ones((2 * width, width), jnp.bfloat16))
        high = total.astype(jnp.bfloat16).astype(jnp.float32)
        extra = jnp.where(lane == 0, high, jnp.where(lane == 1, total - high, 0.0))
        g_ext[h, :, 0:width] = grads
        g_ext[h, :, width:] = extra.astype(jnp.bfloat16)
        l_now[rows, :] = inverse

    def factor_pass(slot):
        vals = jnp.concatenate([win[slot, :, width:], ones], axis=1)
        for h in range(heads):
            rows = slice(h * tok, (h + 1) * tok)
            factor = jnp.exp2(m_buf[slot, rows, :] - m_now[rows, :]) * l_now[rows, :]
            probs = p_buf[slot, rows, :].astype(jnp.float32) * wide(factor)
            prob_grad = dot_nt(g_ext[h], vals)
            ds_buf[slot, rows, :] = (probs * prob_grad).astype(jnp.bfloat16)
            p_buf[slot, rows, :] = probs.astype(jnp.bfloat16)

    halves = (0, 1)

    def part_rows(part):
        return pl.ds(part * width, width)

    def sum_copy(slot, part):
        rows = part_rows(part)
        return remote(
            sib_out.at[slot, rows, sib_rows], sib_in.at[slot, rows], sum_send.at[slot, part], sum_recv.at[slot, part], sibling
        )

    def back_copy(step):
        return remote(
            out_buf.at[step], back_in.at[step], back_send.at[step], back_recv.at[step], (behind(step), core)
        )

    def line_copy(step, part):
        rows = part_rows(part)
        return remote(
            out_buf.at[LINE + step, rows], relay_in.at[step, rows],
            line_send.at[step, part], line_recv.at[step, part], (on_line(-step), core),
        )

    def col_copy(part):
        rows = part_rows(part)
        return remote(
            out_buf.at[LINE, rows], back_in.at[0, rows], col_send.at[part], col_recv.at[part], (me - LINE, core)
        )

    sides = ((1, gt, p_buf), (0, qt, ds_buf))

    def grad_pass(slot):
        for part, left, right in sides:
            total = dot_nn(left[...], right[slot])
            mine[slot, part_rows(part), :] = total
            sib_out[slot, part_rows(part), :] = total.astype(jnp.bfloat16)
            sum_copy(slot, part).start()

    def return_part(slot):
        for part, _, _ in sides:
            rows = part_rows(part)
            sum_copy(slot, part).wait_recv()
            total = mine[slot, rows, my_rows] + sib_in[slot, rows, :].astype(jnp.float32)
            if slot in (0, LINE):
                kept[slot // LINE, rows, :] = total
            else:
                out_buf[slot, rows, :] = total.astype(jnp.bfloat16)
            if slot > LINE:

                @pl.when(has_prev)
                def _():
                    line_copy(slot - LINE, part).start()

        if 0 < slot < LINE:

            @pl.when(exists(slot))
            def _():
                back_copy(slot).start()

    back_order = (6, 5, 7, 3, 2, 1, 4, 0)
    for index in range(WIN + 2):
        if 1 <= index <= WIN:
            grad_pass(back_order[index - 1])
        if index >= 2:
            return_part(back_order[index - 2])
        if index < WIN:
            factor_pass(back_order[index])

    @pl.when(has_prev)
    def _():
        for part, _, _ in sides:
            rows = part_rows(part)
            total = kept[1, rows, :]
            for step in range(1, LINE):
                line_copy(step, part).wait_recv()
                total = total + relay_in[step, rows, :].astype(jnp.float32)
            out_buf[LINE, rows, :] = total.astype(jnp.bfloat16)
            col_copy(part).start()

    for h in range(heads):
        rows = slice(h * tok, (h + 1) * tok)
        total = dot_nn(ds_buf[0, rows, :], win[0, :, 0:width])
        for slot in range(1, WIN):
            total = total + dot_nn(ds_buf[slot, rows, :], win[slot, :, 0:width])
        dq_ref[:, h * width : (h + 1) * width] = (total * scale).astype(jnp.bfloat16)

    for step in range(1, LINE):

        @pl.when(ahead(step) < shards)
        def _():
            back_copy(step).wait_recv()
            kept[0] = kept[0] + back_in[step].astype(jnp.float32)

    for part, _, _ in sides:
        rows = part_rows(part)

        @pl.when(has_next)
        def _():
            col_copy(part).wait_recv()
            kept[0, rows, :] = kept[0, rows, :] + back_in[0, rows, :].astype(jnp.float32)

        if part:
            dv_ref[...] = kept[0, rows, :].T.astype(jnp.bfloat16)
        else:
            dk_ref[...] = (kept[0, rows, :] * scale).T.astype(jnp.bfloat16)

    @pl.when(has_next)
    def _():
        for chunk in range(CHUNKS):
            block_send(LINE, me + LINE, chunk).wait_send()

    for step in range(1, LINE):

        @pl.when(ahead(step) < shards)
        def _():
            for chunk in range(CHUNKS):
                block_send(step, ahead(step), chunk).wait_send()

    @pl.when(has_prev)
    def _():
        for step in range(1, LINE):
            for chunk in range(CHUNKS):
                relay_copy(step, chunk).wait_send()
            for part in halves:
                line_copy(step, part).wait_send()
        for part in halves:
            col_copy(part).wait_send()

    for slot in range(1, WIN):

        @pl.when(exists(slot))
        def _():
            for chunk in range(CHUNKS):
                cross_copy(slot, chunk).wait_send()

    for slot in range(WIN):
        for part in halves:
            sum_copy(slot, part).wait_send()

    for step in range(1, LINE):

        @pl.when(behind(step) >= 0)
        def _():
            back_copy(step).wait_send()


def hand_on(*refs):
    for source, target in zip(refs[:4], refs[4:]):
        target[...] = source[...]


def solution(mesh):
    shards = mesh.shape["ctx"]

    def on_device(queries, keys, values, out_grad, lengths):
        tok, width = keys.shape
        heads = queries.shape[1] // width
        rows = heads * tok
        half = tok // 2
        bf16, f32 = jnp.bfloat16, jnp.float32
        vmem = pl.BlockSpec(memory_space=pltpu.VMEM)
        dma = pltpu.SemaphoreType.DMA
        flops = 6 * 2 * rows * WIN * tok * width
        results = pl.pallas_call(
            functools.partial(kernel, shards, lengths.shape[0]),
            out_shape=(
                jax.ShapeDtypeStruct(queries.shape, bf16),
                jax.ShapeDtypeStruct(queries.shape, bf16),
                jax.ShapeDtypeStruct((half, width), bf16),
                jax.ShapeDtypeStruct((half, width), bf16),
            ),
            in_specs=[pl.BlockSpec(memory_space=pltpu.SMEM)] + [pl.BlockSpec(memory_space=pl.ANY)] * 4,
            out_specs=(vmem,) * 4,
            scratch_shapes=[
                dma((4,)),
                pltpu.VMEM(queries.shape, bf16),
                pltpu.VMEM(queries.shape, bf16),
                pltpu.VMEM((WIN, tok, 2 * width), bf16),
                pltpu.VMEM((WIN, rows, tok), bf16),
                pltpu.VMEM((WIN, rows, tok), bf16),
                pltpu.VMEM((heads, tok, tok), f32),
                pltpu.VMEM((WIN, rows, width), f32),
                pltpu.VMEM((rows, width), f32),
                pltpu.VMEM((rows, width), f32),
                pltpu.VMEM((rows, 2 * width), f32),
                pltpu.VMEM((heads, tok, 2 * width), bf16),
                pltpu.VMEM((heads, tok, 2 * width), bf16),
                pltpu.VMEM((width, rows), bf16),
                pltpu.VMEM((width, rows), bf16),
                pltpu.VMEM((2, 2 * width, half), f32),
                pltpu.VMEM((WIN, 2 * width, tok), f32),
                pltpu.VMEM((WIN, 2 * width, tok), bf16),
                pltpu.VMEM((WIN, 2 * width, half), bf16),
                pltpu.VMEM((WIN, 2 * width, half), bf16),
                pltpu.VMEM((LINE, 2 * width, half), bf16),
                pltpu.VMEM((LINE, 2 * width, half), bf16),
                dma((WIN, CHUNKS)), dma((WIN, CHUNKS)), dma((LINE, CHUNKS)), dma((WIN, CHUNKS)), dma((WIN, CHUNKS)),
                dma((WIN, 2)), dma((WIN, 2)), dma((LINE,)), dma((LINE,)), dma((2,)), dma((2,)),
                dma((LINE, 2)), dma((LINE, 2)),
            ],
            compiler_params=pltpu.CompilerParams(
                collective_id=0, has_side_effects=True, vmem_limit_bytes=56 * 1024 * 1024
            ),
            cost_estimate=pl.CostEstimate(flops=flops, bytes_accessed=1 << 21, transcendentals=rows * WIN * tok),
            name="packed_attention",
        )(lengths, queries, keys, values, out_grad)
        return pl.pallas_call(
            hand_on,
            out_shape=tuple(jax.ShapeDtypeStruct(r.shape, r.dtype) for r in results),
            in_specs=[vmem] * 4,
            out_specs=(vmem,) * 4,
            name="hand_on",
        )(*results)

    return jax.shard_map(
        on_device,
        mesh=mesh,
        in_specs=(P("ctx", "head"), P("ctx", None), P("ctx", None), P("ctx", "head"), P()),
        out_specs=(P("ctx", "head"), P("ctx", "head"), P(("ctx", "head"), None), P(("ctx", "head"), None)),
        check_vma=False,
    )
```
